256 devices in a mesh: rep: 8 (over z_hi, core), ep: 32 (over z_lo, x, y).
Axes of the slice: x: 4, y: 4, z: 8 (z_hi: 4, z_lo: 2; z = z_hi * 2 + z_lo), core: 2. Of those that a mesh axis runs over, the one named last changes fastest.
Arguments:
- expert_inputs: bfloat16 [32, 1024, 1024], P('ep', 'rep'), may hold values from -6 to 6
- expert_cotangent: bfloat16 [32, 1024, 3584], P('ep', 'rep'), may hold values from -0.29882812 to 0.29882812
- row_counts: int32 [32, 8], P('ep', 'rep'), may hold values from 1 to 128, as said below
- expert_master: float32 [32, 1024, 3584], P('ep', 'rep'), may hold values from -6 to 6
- expert_moment: float32 [32, 1024, 3584], P('ep', 'rep'), may hold values from -0.6 to 0.6
- expert_variance: float32 [32, 1024, 3584], P('ep', 'rep'), may hold values from 0.0001 to 1
- layer_inputs: bfloat16 [32768, 7168], P(('rep', 'ep')), may hold values from -24 to 24
- layer_cotangent: bfloat16 [32768, 576], P(('rep', 'ep')), may hold values from -0.059814453 to 0.059814453
- dense_master: float32 [7168, 576], P(('rep', 'ep')), may hold values from -6 to 6
- dense_moment: float32 [7168, 576], P(('rep', 'ep')), may hold values from -0.6 to 0.6
- dense_variance: float32 [7168, 576], P(('rep', 'ep')), may hold values from 0.0001 to 1
Outputs:
- expert_updated: float32 [32, 1024, 3584], P('ep', 'rep')
- dense_updated: float32 [7168, 576], P(('rep', 'ep'))
The draws below stay inside these ranges and needn't reach their ends.
Inputs may be any that keep to these rules, and one draw needn't show every extreme that they name: `row_counts`: live slots of each expert from each replica; some pair has exactly 128 live slots and some pair exactly one.
All inputs are finite; a program needn't handle non-finite values.
Results may differ from the reference program's by a relative error of at most 0.0023.
Values may be sent and summed in bfloat16 or wider, within the bound.
No kernel may reach another device: no remote copies, remote signals or barrier semaphores. Data moves between devices by JAX's collectives and lax.ppermute only.
A program may use at most 128 MiB of HBM per device.

```python
import math
import jax
import jax.numpy as jnp
from jax import lax

D = 7168
DW = 3584
HID = 1024
KV = 576
CAP = 128
EXPERTS = 32
REPLICAS = 8
SLOTS = 1024
TOKENS = 32768


def draw_row_counts(key, part):
    key = jax.random.fold_in(key, 7)
    key_values, key_high, key_low = jax.random.split(key, 3)
    entries = EXPERTS * REPLICAS
    counts = jax.random.randint(key_values, (entries,), 1, CAP + 1)
    high_spot = jax.random.randint(key_high, (), 0, entries)
    low_spot = (high_spot + jax.random.randint(key_low, (), 1, entries)) % entries
    positions = jnp.arange(entries)
    counts = jnp.where(positions == high_spot, CAP, counts)
    counts = jnp.where(positions == low_spot, 1, counts)
    return counts.reshape(EXPERTS, REPLICAS).astype(jnp.int32)


def spiked(values, own_key, source, target, blocks, factor):
    owner, partner = [(jnp.arange(values.shape[dim]) // (values.shape[dim] // blocks)).reshape([-1 if axis == dim else 1 for axis in range(values.ndim)]) for dim in (source, target)]
    chosen = jax.random.permutation(own_key, blocks)[partner]
    strong = (owner == chosen) | (owner == (partner + blocks // 2) % blocks)
    return jnp.where(strong, factor * values, values)


def block_levels(own_key, extent, cuts, low, high):
    loudness = 1.0
    for axis_at, shards_of in cuts:
        steps = jax.random.uniform(jax.random.fold_in(jax.random.fold_in(own_key, 6), axis_at), (shards_of,), jnp.float32, low / len(cuts), high / len(cuts))
        loudness = loudness * jnp.repeat(jnp.exp(steps), extent[axis_at] // shards_of).reshape((-1,) + (1,) * (len(extent) - 1 - axis_at))
    return loudness


def normal_values(rng, shape, scale, bound, cuts=(), dtype=jnp.bfloat16):
    values = scale * jax.random.normal(rng, shape, jnp.float32)
    if cuts:
        values = values * block_levels(rng, shape, cuts, -0.22, 0.18)
    return jnp.clip(values, -bound, bound).astype(dtype)


def gaussian_with(stream_key, extent, deviation, reach, cuts, heavy, held_as=jnp.bfloat16):
    array = deviation * jax.random.normal(stream_key, extent, jnp.float32)
    if cuts:
        array = array * block_levels(stream_key, extent, cuts, -0.22, 0.18)
    return jnp.clip(spiked(array, jax.random.fold_in(stream_key, 3), *heavy), -reach, reach).astype(held_as)


def setup_inputs(seed: int = 0) -> dict:
    streams_of = jax.random.split(jax.random.key(seed), 12)
    return {
        "expert_inputs": gaussian_with(streams_of[0], (EXPERTS, SLOTS, HID), 1.0, 6.0, ((0, 32), (1, 8)), (1, 2, 8, 2.0)),
        "expert_cotangent": normal_values(streams_of[1], (EXPERTS, SLOTS, DW), 0.05, 0.29882812, ((0, 32), (1, 8))),
        "row_counts": draw_row_counts(jax.random.fold_in(streams_of[11], 71), 0),
        "expert_master": normal_values(streams_of[3], (EXPERTS, HID, DW), 1.0, 6.0, ((0, 32), (1, 8)), jnp.float32),
        "expert_moment": normal_values(streams_of[4], (EXPERTS, HID, DW), 0.1, 0.6, ((0, 32), (1, 8)), jnp.float32),
        "expert_variance": jnp.clip(jnp.exp(math.log(1.0) - 9.2103404 * jax.random.uniform(streams_of[5], (EXPERTS, HID, DW), jnp.float32) ** block_levels(streams_of[5], (EXPERTS, HID, DW), ((0, 32), (1, 8)), -0.2, 0.2)), 0.0001, 1.0),
        "layer_inputs": gaussian_with(streams_of[6], (TOKENS, D), 1.0, 24.0, ((0, 256),), (0, 1, 256, 6.0)),
        "layer_cotangent": normal_values(streams_of[7], (TOKENS, KV), 0.01, 0.059814453, ((0, 256),)),
        "dense_master": normal_values(streams_of[8], (D, KV), 1.0, 6.0, ((0, 256),), jnp.float32),
        "dense_moment": normal_values(streams_of[9], (D, KV), 0.1, 0.6, ((0, 256),), jnp.float32),
        "dense_variance": jnp.clip(jnp.exp(math.log(1.0) - 9.2103404 * jax.random.uniform(streams_of[10], (D, KV), jnp.float32) ** block_levels(streams_of[10], (D, KV), ((0, 256),), -0.2, 0.2)), 0.0001, 1.0),
    }


beta_first = 0.9
beta_second = 0.999
step_count = 1000.0
learn_rate = 0.05
weight_decay = 0.1
epsilon = 1e-08

def adam_step(master, moment, variance, gradient):
    moment_new = beta_first * moment + (1.0 - beta_first) * gradient
    variance_new = beta_second * variance + (1.0 - beta_second) * gradient * gradient
    first_fix = 1.0 - beta_first ** step_count
    second_fix = 1.0 - beta_second ** step_count
    update = moment_new / first_fix / (jnp.sqrt(variance_new / second_fix) + epsilon)
    return master - learn_rate * (update + weight_decay * master)

def transpose_product(left, right):
    return lax.dot_general(left, right, (((0,), (0,)), ((), ())), preferred_element_type=jnp.float32)

def expert_gradient(triple):
    inputs_one, cotangent_one, counts_one = triple
    inputs_split = inputs_one.reshape(REPLICAS, CAP, HID)
    cotangent_split = cotangent_one.reshape(REPLICAS, CAP, DW)
    live_rows = jnp.arange(CAP)[None, :] < counts_one[:, None]
    masked = jnp.where(live_rows[:, :, None], cotangent_split, jnp.zeros_like(cotangent_split))

    def accumulate(running, pair):
        partial_value = transpose_product(pair[0], pair[1])
        rounded = lax.optimization_barrier(partial_value.astype(jnp.bfloat16)).astype(jnp.float32)
        return (running + rounded, None)
    summed, unused = lax.scan(accumulate, jnp.zeros((HID, DW), jnp.float32), (inputs_split, masked))
    return summed

def reference(expert_inputs, expert_cotangent, row_counts, expert_master, expert_moment, expert_variance, layer_inputs, layer_cotangent, dense_master, dense_moment, dense_variance):
    expert_grad = lax.map(expert_gradient, (expert_inputs, expert_cotangent, row_counts))
    expert_updated = adam_step(expert_master, expert_moment, expert_variance, expert_grad)
    dense_grad = transpose_product(layer_inputs, layer_cotangent)
    dense_updated = adam_step(dense_master, dense_moment, dense_variance, dense_grad)
    return (expert_updated, dense_updated)
```

```python
import functools
import jax
import jax.numpy as jnp
import numpy as np
from jax import lax
from jax.experimental import pallas as pl
from jax.experimental.pallas import tpu as pltpu
from jax.sharding import Mesh, PartitionSpec as P

beta_first = 0.9
beta_second = 0.999
step_count = 1000.0
learn_rate = 0.05
weight_decay = 0.1
epsilon = 1e-08

SLOT = 128
HID = 1024
DW = 3584
HALF = 1792
D = 7168
KV = 576
PART = 896
ROWS = 28
PAD = 32
bf16, f32 = jnp.bfloat16, jnp.float32

PAIR_A = [(0, 1), (1, 0), (2, 3), (3, 2)]
PAIR_B = [(0, 3), (3, 0), (1, 2), (2, 1)]
VMEM = 48 * 1024 * 1024


def adam_step(master, moment, variance, gradient):
    moment_new = beta_first * moment + (1.0 - beta_first) * gradient
    variance_new = beta_second * variance + (1.0 - beta_second) * gradient * gradient
    first_fix = 1.0 - beta_first**step_count
    second_fix = 1.0 - beta_second**step_count
    update = moment_new / first_fix / (jnp.sqrt(variance_new / second_fix) + epsilon)
    return master - learn_rate * (update + weight_decay * master)


def dot0(left, right):
    return lax.dot_general(left, right, (((0,), (0,)), ((), ())), preferred_element_type=f32)


def pack_kernel(where, hid_ref, cot_ref, to_a_ref, to_b_ref, own_ref, masked):
    j, core, count = where[0], where[1], where[2]
    other = 1 - core
    near_a = j + 1 - 2 * lax.rem(j, 2)
    near_b = 3 - j
    across = lax.rem(j + 2, 4)
    live = lax.broadcasted_iota(jnp.int32, (SLOT, HID), 0) < count
    masked[...] = jnp.where(live, hid_ref[...], jnp.zeros_like(hid_ref))

    def block(chip, which):
        start = pl.multiple_of((chip * 2 + which) * 128, 128)
        return masked[:, pl.ds(start, 128)]

    to_a_ref[:, :HALF] = cot_ref[:, :HALF]
    to_b_ref[:, :HALF] = cot_ref[:, HALF:]
    for ref, near in ((to_a_ref, near_a), (to_b_ref, near_b)):
        for n, (chip, which) in enumerate(
            ((near, core), (across, core), (near, other), (across, other))
        ):
            ref[:, HALF + n * 128 : HALF + (n + 1) * 128] = block(chip, which)
    for n, chip in enumerate((j, near_b, j, near_a)):
        own_ref[:, n * 128 : (n + 1) * 128] = block(chip, core)


def sibling_kernel(where, hid_ref, cot_ref, out_ref, masked):
    j, core, count = where[0], where[1], where[2]
    other = 1 - core
    near_a = j + 1 - 2 * lax.rem(j, 2)
    near_b = 3 - j
    live = lax.broadcasted_iota(jnp.int32, (SLOT, HID), 0) < count
    masked[...] = jnp.where(live, hid_ref[...], jnp.zeros_like(hid_ref))
    out_ref[:, :DW] = cot_ref[...]
    for n, chip in enumerate((j, near_b, j, near_a)):
        start = pl.multiple_of((chip * 2 + other) * 128, 128)
        out_ref[:, DW + n * 128 : DW + (n + 1) * 128] = masked[:, pl.ds(start, 128)]


def dense_pack_kernel(where, lay_ref, cot_ref, out_ref):
    other = 1 - where[1]
    for n in range(4):
        start = pl.multiple_of((2 * n + other) * PART, 128)
        out_ref[:, n * PART : (n + 1) * PART] = lay_ref[:, pl.ds(start, PART)]
    out_ref[:, 4 * PART : 4 * PART + KV] = cot_ref[...]
    out_ref[:, 4 * PART + KV :] = jnp.zeros((SLOT, 64), bf16)


def whole(shape):
    return pl.BlockSpec(shape, lambda *_: (0,) * len(shape))


def packing(kernel, where, args, widths, scratch):
    outs = [jax.ShapeDtypeStruct((SLOT, w), bf16) for w in widths]
    return pl.pallas_call(
        kernel,
        out_shape=outs,
        grid_spec=pltpu.PrefetchScalarGridSpec(
            num_scalar_prefetch=1,
            grid=(1,),
            in_specs=[whole(a.shape) for a in args],
            out_specs=[whole(o.shape) for o in outs],
            scratch_shapes=scratch,
        ),
        compiler_params=pltpu.CompilerParams(vmem_limit_bytes=VMEM),
    )(where, *args)


def products_kernel(
    own_ca, own_cb, own_ha, own_hb, sib_ca, sib_cb, sib_ha, sib_hb,
    far_ca, far_ha, far_cb, far_hb, sf_ca, sf_ha, sf_cb, sf_hb,
    send_a, send_b, keep,
):
    for n, (h, c, send) in enumerate((
        ((own_ha, sib_ha, far_ha, sf_ha), (own_ca, sib_ca, far_ca, sf_ca), send_a),
        ((own_hb, sib_hb, far_hb, sf_hb), (own_cb, sib_cb, far_cb, sf_cb), send_b),
    )):
        left = jnp.concatenate([r[...] for r in h], axis=0)
        right = jnp.concatenate([r[...] for r in c], axis=0)
        result = dot0(left, right)
        keep[n] = result[:SLOT]
        send[...] = result[SLOT:].astype(bf16)


def expert_products(cot, own, sib, far_a, far_b, sib_far):
    def at(fixed):
        return pl.BlockSpec((SLOT, 256), lambda i: (0, fixed))

    def tile(first):
        return pl.BlockSpec((SLOT, 256), lambda i: (0, first + i))

    return pl.pallas_call(
        products_kernel,
        grid=(7,),
        out_shape=[
            jax.ShapeDtypeStruct((SLOT, HALF), bf16),
            jax.ShapeDtypeStruct((SLOT, HALF), bf16),
            jax.ShapeDtypeStruct((2, SLOT, HALF), f32),
        ],
        in_specs=[
            tile(0), tile(7), at(0), at(1),
            tile(0), tile(7), at(14), at(15),
            tile(0), at(7), tile(0), at(7),
            tile(0), at(7), tile(8), at(15),
        ],
        out_specs=[tile(0), tile(0), pl.BlockSpec((2, SLOT, 256), lambda i: (0, 0, i))],
        compiler_params=pltpu.CompilerParams(vmem_limit_bytes=VMEM),
    )(cot, cot, own, own, sib, sib, sib, sib, far_a, far_a, far_b, far_b,
      sib_far, sib_far, sib_far, sib_far)


def expert_adam_kernel(keep, got_a, got_b, master, moment, variance, out):
    half = pl.program_id(0)

    def go(got):
        gradient = keep[0] + got[...].astype(f32)
        out[...] = adam_step(master[...], moment[...], variance[...], gradient)

    @pl.when(half == 0)
    def _():
        go(got_a)

    @pl.when(half == 1)
    def _():
        go(got_b)


def expert_adam(keep, got_a, got_b, master, moment, variance):
    wide = pl.BlockSpec((SLOT, 256), lambda h, i: (0, h * 7 + i))
    return pl.pallas_call(
        expert_adam_kernel,
        grid=(2, 7),
        out_shape=jax.ShapeDtypeStruct((SLOT, DW), f32),
        in_specs=[
            pl.BlockSpec((1, SLOT, 256), lambda h, i: (h, 0, i)),
            pl.BlockSpec((SLOT, 256), lambda h, i: (0, jnp.where(h == 0, i, 6))),
            pl.BlockSpec((SLOT, 256), lambda h, i: (0, jnp.where(h == 0, 0, i))),
            wide, wide, wide,
        ],
        out_specs=wide,
        compiler_params=pltpu.CompilerParams(vmem_limit_bytes=VMEM),
    )(keep, got_a, got_b, master, moment, variance)


def row_sources():
    table = np.full((2, 1024), -1, np.int32)
    for first in range(4):
        for second in range(4):
            for low in range(2):
                for row in range(ROWS):
                    place = ((first * 4 + second) * 2 + low) * PAD + row
                    table[0, place] = low * 448 + first * 112 + second * 28 + row
                    table[1, place] = low * 448 + second * 112 + first * 28 + row
    return table[:, :, None]


def dense_kernel(where, lay_ref, cot_ref, got_ref, src_ref, out_ref, order):
    n = pl.program_id(0)

    @pl.when(n == 0)
    def _():
        columns = lax.broadcasted_iota(jnp.int32, (1024, PART), 1)
        order[...] = jnp.where(columns == src_ref[0], 1.0, 0.0).astype(bf16)

    start = pl.multiple_of(n * PART, 128)
    tokens = jnp.concatenate([lay_ref[...], got_ref[:, pl.ds(start, PART)]], axis=0)
    grads = jnp.concatenate([cot_ref[...], got_ref[:, 4 * PART : 4 * PART + KV]], axis=0)
    moved = lax.dot_general(
        order[...], tokens, (((1,), (1,)), ((), ())), preferred_element_type=f32
    ).astype(bf16)
    out_ref[0] = jnp.dot(moved, grads, preferred_element_type=f32).astype(bf16)


def dense_product(where, lay, cot, got):
    sources = jnp.asarray(row_sources())
    return pl.pallas_call(
        dense_kernel,
        out_shape=jax.ShapeDtypeStruct((4, 1024, KV), bf16),
        grid_spec=pltpu.PrefetchScalarGridSpec(
            num_scalar_prefetch=1,
            grid=(4,),
            in_specs=[
                pl.BlockSpec((SLOT, PART), lambda n, w: (0, 2 * n + w[1])),
                whole(cot.shape),
                whole(got.shape),
                pl.BlockSpec((1, 1024, 1), lambda n, w: (w[1], 0, 0)),
            ],
            out_specs=pl.BlockSpec((1, 1024, KV), lambda n, w: (n, 0, 0)),
            scratch_shapes=[pltpu.VMEM((1024, PART), bf16)],
        ),
        compiler_params=pltpu.CompilerParams(vmem_limit_bytes=VMEM),
    )(where, lay, cot, got, sources)


def plane_pairs(stage, step):
    pairs = []
    for core in range(2):
        for x in range(4):
            for y in range(4):
                along_x = (core + stage) % 2 == 0
                to = ((x + step) % 4, y) if along_x else (x, (y + step) % 4)
                pairs.append((core * 16 + x * 4 + y, core * 16 + to[0] * 4 + to[1]))
    return pairs


def ring_scatter(blocks, me, stage):
    axes = ("co", "x", "y")

    def take(place, first, last):
        return lax.dynamic_index_in_dim(blocks[first:last], place, axis=1, keepdims=False)

    up, down, across = (me + 1) % 4, (me + 3) % 4, (me + 2) % 4
    rise, fall = plane_pairs(stage, 1), plane_pairs(stage, -1)
    got_up = lax.ppermute(take(across, 0, 2).astype(bf16), axes, rise)
    got_down = lax.ppermute(take(across, 2, 4).astype(bf16), axes, fall)
    to_up = jnp.concatenate(
        [
            (take(up, 0, 2).astype(f32) + got_up.astype(f32)).astype(bf16),
            take(up, 2, 4).astype(bf16),
        ]
    )
    to_down = jnp.concatenate(
        [
            take(down, 0, 2).astype(bf16),
            (take(down, 2, 4).astype(f32) + got_down.astype(f32)).astype(bf16),
        ]
    )
    from_low = lax.ppermute(to_up, axes, rise)
    from_high = lax.ppermute(to_down, axes, fall)
    return take(me, 0, 4).astype(f32) + from_low.astype(f32) + from_high.astype(f32)


def on_device(
    expert_inputs,
    expert_cotangent,
    row_counts,
    expert_master,
    expert_moment,
    expert_variance,
    layer_inputs,
    layer_cotangent,
    dense_master,
    dense_moment,
    dense_variance,
):
    j, core = lax.axis_index("zh"), lax.axis_index("co")
    low, x, y = lax.axis_index("zl"), lax.axis_index("x"), lax.axis_index("y")
    where = jnp.stack([j, core, row_counts[0, 0]]).astype(jnp.int32)
    hid, cot = expert_inputs[0], expert_cotangent[0]
    swap = [(0, 1), (1, 0)]

    to_a, to_b, own = packing(
        pack_kernel, where, (hid, cot), (2304, 2304, 512), [pltpu.VMEM((SLOT, HID), bf16)]
    )
    far_a = lax.ppermute(to_a, "zh", PAIR_A)
    far_b = lax.ppermute(to_b, "zh", PAIR_B)

    (to_core,) = packing(dense_pack_kernel, where, (layer_inputs, layer_cotangent), (4224,), [])
    dense_got = lax.ppermute(to_core, "co", swap)
    (to_sib,) = packing(
        sibling_kernel, where, (hid, cot), (4096,), [pltpu.VMEM((SLOT, HID), bf16)]
    )
    sib = lax.ppermute(to_sib, "co", swap)
    product = dense_product(where, layer_inputs, layer_cotangent, dense_got)

    first = jnp.where(core == 0, x, y)
    second = jnp.where(core == 0, y, x)
    plane = ring_scatter(product.reshape(4, 4, 256, KV), first, 0)
    line = ring_scatter(plane.reshape(4, 4, 64, KV), second, 1)

    sib_far = lax.ppermute(
        jnp.concatenate(
            [far_a[:, :HALF], far_a[:, 2048:], far_b[:, :HALF], far_b[:, 2048:]], axis=1
        ),
        "co",
        swap,
    )
    send_a, send_b, keep = expert_products(cot, own, sib, far_a, far_b, sib_far)
    got_a = lax.ppermute(send_a, "zh", PAIR_B)
    got_b = lax.ppermute(send_b, "zh", PAIR_A)

    line = line.reshape(4, 2, PAD, KV)
    mine = lax.dynamic_index_in_dim(line, low, axis=1, keepdims=False)
    theirs = lax.dynamic_index_in_dim(line, 1 - low, axis=1, keepdims=False)
    mine = mine + lax.ppermute(theirs.astype(bf16), "zl", swap).astype(f32)
    dense_grad = lax.dynamic_index_in_dim(mine, j, keepdims=False)
    for step in (1, 2, 3):
        out = lax.dynamic_index_in_dim(mine, (j + step) % 4, keepdims=False).astype(bf16)
        got = lax.ppermute(out, "zh", [(i, (i + step) % 4) for i in range(4)])
        dense_grad = dense_grad + got.astype(f32)
    dense_updated = adam_step(dense_master, dense_moment, dense_variance, dense_grad[:ROWS])

    expert_updated = expert_adam(
        keep, got_a, got_b, expert_master[0], expert_moment[0], expert_variance[0]
    )
    return (expert_updated[None], dense_updated)


def solution(mesh):
    fine = Mesh(mesh.devices.reshape(4, 2, 2, 4, 4), ("zh", "co", "zl", "x", "y"))
    ep, rep = ("zl", "x", "y"), ("zh", "co")
    expert = P(ep, rep, None)
    dense = P(rep + ep, None)
    in_specs = (expert, expert, P(ep, rep)) + (expert,) * 3 + (dense,) * 5
    return jax.shard_map(
        on_device, mesh=fine, in_specs=in_specs, out_specs=(expert, dense), check_vma=False
    )
```

```python
import functools
import jax
import jax.numpy as jnp
from jax import lax
from jax.experimental import pallas as pl
from jax.experimental.pallas import tpu as pltpu
from jax.sharding import Mesh, PartitionSpec as P

beta_first = 0.9
beta_second = 0.999
step_count = 1000.0
learn_rate = 0.05
weight_decay = 0.1
epsilon = 1e-08

SLOT = 128
HID = 1024
DW = 3584
HALF = 1792
TILE = 896
D = 7168
KV = 576
PART = 896
ROWS = 28
PAD = 32
bf16, f32 = jnp.bfloat16, jnp.float32

PAIR_A = [(0, 1), (1, 0), (2, 3), (3, 2)]
PAIR_B = [(0, 3), (3, 0), (1, 2), (2, 1)]
VMEM = 24 * 1024 * 1024
ADAM_COST = pl.CostEstimate(flops=20_000_000, bytes_accessed=10_000_000, transcendentals=0)
FAR_COST = pl.CostEstimate(flops=6_000_000_000, bytes_accessed=4_000_000, transcendentals=0)


def adam_step(master, moment, variance, gradient):
    moment_new = beta_first * moment + (1.0 - beta_first) * gradient
    variance_new = beta_second * variance + (1.0 - beta_second) * gradient * gradient
    first_fix = 1.0 - beta_first**step_count
    second_fix = 1.0 - beta_second**step_count
    update = moment_new / first_fix / (jnp.sqrt(variance_new / second_fix) + epsilon)
    return master - learn_rate * (update + weight_decay * master)


def dot0(left, right):
    return lax.dot_general(left, right, (((0,), (0,)), ((), ())), preferred_element_type=f32)


def spot_of(*axes):
    return tuple(lax.axis_index(a) for a in axes)


def masked_blocks(counts, hid_ref, masked):
    live = lax.broadcasted_iota(jnp.int32, (SLOT, HID), 0) < counts[0, 0]
    masked[...] = jnp.where(live, hid_ref[...], jnp.zeros_like(hid_ref))

    def block(chip, which):
        start = pl.multiple_of((chip * 2 + which) * 128, 128)
        return masked[:, pl.ds(start, 128)]

    return block


def nearest(j):
    return j + 1 - 2 * lax.rem(j, 2), 3 - j, lax.rem(j + 2, 4)


def pack_kernel(counts, hid_ref, cot_ref, to_a, to_b, own_ref, masked, sems):
    j, core = spot_of("zh", "co")
    other = 1 - core
    near_a, near_b, across = nearest(j)
    copies = [
        pltpu.make_async_copy(
            cot_ref.at[:, n * HALF : (n + 1) * HALF], to.at[:, :HALF], sems.at[n]
        )
        for n, to in enumerate((to_a, to_b))
    ]
    for copy in copies:
        copy.start()
    block = masked_blocks(counts, hid_ref, masked)
    for to, near in ((to_a, near_a), (to_b, near_b)):
        for n, (chip, which) in enumerate(
            ((near, core), (across, core), (near, other), (across, other))
        ):
            to[:, HALF + n * 128 : HALF + (n + 1) * 128] = block(chip, which)
    for n, chip in enumerate((j, near_b, j, near_a)):
        own_ref[:, n * 128 : (n + 1) * 128] = block(chip, core)
    for copy in copies:
        copy.wait()


def sibling_kernel(counts, hid_ref, cot_ref, out_ref, masked, sems):
    j, core = spot_of("zh", "co")
    near_a, near_b, _ = nearest(j)
    copy = pltpu.make_async_copy(cot_ref, out_ref.at[:, :DW], sems.at[0])
    copy.start()
    block = masked_blocks(counts, hid_ref, masked)
    for n, chip in enumerate((j, near_b, j, near_a)):
        out_ref[:, DW + n * 128 : DW + (n + 1) * 128] = block(chip, 1 - core)
    copy.wait()


def dense_pack_kernel(lay_ref, cot_ref, out_ref, own_ref, cot, sems):
    j, core = spot_of("zh", "co")
    last = pltpu.make_async_copy(cot_ref, cot, sems.at[8])
    last.start()
    copies = []
    for n in range(4):
        for m, (ref, side) in enumerate(((out_ref, 1 - core), (own_ref, core))):
            start = pl.multiple_of((2 * lax.rem(j + n, 4) + side) * PART, 128)
            copies.append(
                pltpu.make_async_copy(
                    lay_ref.at[:, pl.ds(start, PART)],
                    ref.at[:, n * PART : (n + 1) * PART],
                    sems.at[2 * n + m],
                )
            )
    for copy in copies[::2] + copies[1::2]:
        copy.start()
    last.wait()
    out_ref[:, 4 * PART : 4 * PART + KV] = cot[...].T
    out_ref[:, 4 * PART + KV :] = jnp.zeros((SLOT, 64), bf16)
    for copy in copies:
        copy.wait()


def whole(shape):
    return pl.BlockSpec(shape, lambda *_: (0,) * len(shape))


def in_vmem(kernel, outs, *args, scratch=(), far=(), vmem=VMEM, cost=None):
    specs = [
        pl.BlockSpec(
            memory_space=pltpu.SMEM if a.dtype == jnp.int32 else pltpu.HBM if n in far else pltpu.VMEM
        )
        for n, a in enumerate(args)
    ]
    return pl.pallas_call(
        kernel,
        out_shape=[jax.ShapeDtypeStruct(shape, dtype) for shape, dtype in outs],
        in_specs=specs,
        out_specs=[pl.BlockSpec(memory_space=pltpu.VMEM)] * len(outs),
        scratch_shapes=scratch,
        cost_estimate=cost,
        compiler_params=pltpu.CompilerParams(vmem_limit_bytes=vmem),
    )(*args)


def far_kernel(near_a, near_b, out):
    for n, near in enumerate((near_a, near_b)):
        at = n * (HALF + 256)
        out[:, at : at + HALF] = near[:, :HALF]
        out[:, at + HALF : at + HALF + 256] = near[:, HALF + 256 :]


def products_kernel(cot, own, sib, near_a, near_b, far, a0, a1, b0, b1, keep):
    for n, (near, sends) in enumerate(((near_a, (a0, a1)), (near_b, (b0, b1)))):
        at = n * HALF
        there = n * (HALF + 256)
        h = jnp.concatenate(
            [
                own[:, n * 256 : n * 256 + 256],
                sib[:, DW + n * 256 : DW + n * 256 + 256],
                near[:, HALF : HALF + 256],
                far[:, there + HALF : there + HALF + 256],
            ]
        )
        c = jnp.concatenate(
            [cot[:, at : at + HALF], sib[:, at : at + HALF], near[:, :HALF],
             far[:, there : there + HALF]]
        )
        result = dot0(h, c)
        keep[n] = result[:SLOT]
        for i, send in enumerate(sends):
            send[...] = result[SLOT:, i * TILE : (i + 1) * TILE].astype(bf16)


def expert_products(*args):
    outs = [((SLOT, TILE), bf16)] * 4 + [((2, SLOT, HALF), f32)]
    return in_vmem(products_kernel, outs, *args)


def expert_adam_kernel(keep, a0, a1, b0, b1, master, moment, variance, out):
    for n, got in enumerate((a0, a1, b0, b1)):

        @pl.when(pl.program_id(0) == n)
        def _(got=got):
            gradient = keep[0] + got[...].astype(f32)
            out[...] = adam_step(master[...], moment[...], variance[...], gradient)


def expert_adam(keep, got, master, moment, variance):
    wide = pl.BlockSpec((SLOT, TILE), lambda n: (0, n))
    return pl.pallas_call(
        expert_adam_kernel,
        grid=(4,),
        out_shape=jax.ShapeDtypeStruct((SLOT, DW), f32),
        in_specs=[
            pl.BlockSpec((1, SLOT, TILE), lambda n: (n // 2, 0, n % 2)),
            *[pl.BlockSpec((SLOT, TILE), lambda n: (0, 0))] * 4,
            wide, wide, wide,
        ],
        out_specs=wide,
        cost_estimate=ADAM_COST,
        compiler_params=pltpu.CompilerParams(vmem_limit_bytes=VMEM),
    )(keep, *got, master, moment, variance)


def order_kernel(order):
    core, low, x, y = spot_of("co", "zl", "x", "y")
    place = lax.broadcasted_iota(jnp.int32, (1, 1024), 1)
    first = (place // 256 + x + core * (y - x)) % 4
    second = (place // 64 % 4 + y + core * (x - y)) % 4
    half = (place // 32 % 2 + low) % 2
    row = place % PAD
    spot = half * 448 + first * (112 - 84 * core) + second * (28 + 84 * core) + row
    spot = jnp.where(row < ROWS, spot, -1)
    rows = lax.broadcasted_iota(jnp.int32, (PART, 1024), 0)
    order[...] = jnp.where(rows == spot, 1.0, 0.0).astype(bf16)


def permute_kernel(order, own, to_core, got, *outs):
    for n in range(4):
        part = slice(n * PART, (n + 1) * PART)
        tokens = jnp.concatenate([own[:, part], got[:, part]])
        moved = jnp.dot(tokens, order[...], preferred_element_type=f32).astype(bf16)
        for k, out in enumerate(outs):
            out[:, n * 256 : n * 256 + 256] = moved[:, k * 256 : k * 256 + 256]
    for out in outs:
        out[:SLOT, 1024:] = to_core[:, 4 * PART :]
        out[SLOT:, 1024:] = got[:, 4 * PART :]


def dense_product_kernel(b0, b1, b2, b3, keep, up, across, down):
    blocks = (b0, b1, b2, b3)
    grads = jnp.concatenate([b[:, 1024 : 1024 + KV] for b in blocks])
    for n in range(4):
        tokens = jnp.concatenate([b[:, n * 256 : n * 256 + 256] for b in blocks])
        result = dot0(tokens, grads)
        keep[n] = result[:64]
        for k, out in enumerate((up, across, down)):
            out[n] = result[64 * k + 64 : 64 * k + 128].astype(bf16)


def plane_pairs(stage, step):
    pairs = []
    for core in range(2):
        for x in range(4):
            for y in range(4):
                along_x = (core + stage) % 2 == 0
                to = ((x + step) % 4, y) if along_x else (x, (y + step) % 4)
                pairs.append((core * 16 + x * 4 + y, core * 16 + to[0] * 4 + to[1]))
    return pairs


def add(*terms):
    return functools.reduce(lambda a, b: a + b, [t.astype(f32) for t in terms])


def tie(values, *others):
    return lax.optimization_barrier((values, others))[0]


def on_device(
    expert_inputs,
    expert_cotangent,
    row_counts,
    expert_master,
    expert_moment,
    expert_variance,
    layer_inputs,
    layer_cotangent,
    dense_master,
    dense_moment,
    dense_variance,
):
    hid, cot = expert_inputs[0], expert_cotangent[0]
    swap = [(0, 1), (1, 0)]

    (order,) = in_vmem(order_kernel, [((PART, 1024), bf16)])
    to_core, own_part = in_vmem(
        dense_pack_kernel,
        [((SLOT, 4224), bf16), ((SLOT, 4 * PART), bf16)],
        layer_inputs,
        layer_cotangent.T,
        scratch=[pltpu.VMEM((KV, SLOT), bf16), pltpu.SemaphoreType.DMA((9,))],
        far=(0, 1),
        vmem=56 * 1024 * 1024,
    )
    dense_got = lax.ppermute(to_core, "co", swap)

    to_a, to_b, own = in_vmem(
        pack_kernel,
        [((SLOT, w), bf16) for w in (2304, 2304, 512)],
        row_counts,
        hid,
        cot,
        scratch=[pltpu.VMEM((SLOT, HID), bf16), pltpu.SemaphoreType.DMA((2,))],
        far=(2,),
    )
    near_a = lax.ppermute(to_a, "zh", PAIR_A)
    near_b = lax.ppermute(to_b, "zh", PAIR_B)
    (to_sib,) = in_vmem(
        sibling_kernel,
        [((SLOT, DW + 512), bf16)],
        row_counts,
        hid,
        cot,
        scratch=[pltpu.VMEM((SLOT, HID), bf16), pltpu.SemaphoreType.DMA((1,))],
        far=(2,),
    )
    sib = lax.ppermute(to_sib, "co", swap)

    axes = ("co", "x", "y")
    blocks = list(
        in_vmem(permute_kernel, [((256, 1664), bf16)] * 4, order, own_part, to_core, dense_got)
    )
    blocks = [blocks[0]] + [
        lax.ppermute(blocks[step], axes, plane_pairs(0, step)) for step in (2, 1, 3)
    ]
    keep, up, across, down = in_vmem(
        dense_product_kernel, [((4, 64, KV), f32)] + [((4, 64, KV), bf16)] * 3, *blocks
    )

    (to_far,) = in_vmem(
        far_kernel, [((SLOT, DW + 512), bf16)], near_a, near_b, cost=FAR_COST
    )
    far = lax.ppermute(tie(to_far, *blocks[1:]), "co", swap)
    a0, a1, b0, b1, mine_too = expert_products(cot, own, sib, near_a, near_b, far)
    sums = [
        lax.ppermute(send, "zh", pairs)
        for send, pairs in ((a0, PAIR_B), (a1, PAIR_B), (b0, PAIR_A), (b1, PAIR_A))
    ]

    up, across, down = tie((up, across, down), a0)
    terms = [
        lax.ppermute(block, axes, plane_pairs(1, step))
        for step, block in ((2, across), (1, up), (3, down))
    ]

    line = add(tie(keep, sums[0], sums[2]), *terms).reshape(4, 2, PAD, KV)
    mine = line[:, 0] + lax.ppermute(line[:, 1].astype(bf16), "zl", swap).astype(f32)
    dense_grad = mine[0]
    for step in (2, 1, 3):
        got = lax.ppermute(mine[step].astype(bf16), "zh", [(i, (i + step) % 4) for i in range(4)])
        dense_grad = dense_grad + got.astype(f32)
    dense_updated = adam_step(dense_master, dense_moment, dense_variance, dense_grad[:ROWS])

    expert_updated = expert_adam(
        mine_too, sums, expert_master[0], expert_moment[0], expert_variance[0]
    )
    return (expert_updated[None], dense_updated)


def solution(mesh):
    fine = Mesh(mesh.devices.reshape(4, 2, 2, 4, 4), ("zh", "co", "zl", "x", "y"))
    ep, rep = ("zl", "x", "y"), ("zh", "co")
    expert = P(ep, rep, None)
    dense = P(rep + ep, None)
    in_specs = (expert, expert, P(ep, rep)) + (expert,) * 3 + (dense,) * 5
    return jax.shard_map(
        on_device, mesh=fine, in_specs=in_specs, out_specs=(expert, dense), check_vma=False
    )
```

```python
import functools
import jax
import jax.numpy as jnp
from jax import lax
from jax.experimental import pallas as pl
from jax.experimental.pallas import tpu as pltpu
from jax.sharding import Mesh, PartitionSpec as P

beta_first = 0.9
beta_second = 0.999
step_count = 1000.0
learn_rate = 0.05
weight_decay = 0.1
epsilon = 1e-08

SLOT = 128
HID = 1024
DW = 3584
HALF = 1792
LEAD = 896
REST = HALF - LEAD
D = 7168
KV = 576
PART = 896
ROWS = 28
PAD = 32
bf16, f32 = jnp.bfloat16, jnp.float32

PAIR_A = [(0, 1), (1, 0), (2, 3), (3, 2)]
PAIR_B = [(0, 3), (3, 0), (1, 2), (2, 1)]
VMEM = 24 * 1024 * 1024
LONG = pl.CostEstimate(flops=10_000_000_000, bytes_accessed=4_000_000, transcendentals=0)
FAR_COST = pl.CostEstimate(flops=6_000_000_000, bytes_accessed=4_000_000, transcendentals=0)


def adam_step(master, moment, variance, gradient):
    moment_new = beta_first * moment + (1.0 - beta_first) * gradient
    variance_new = beta_second * variance + (1.0 - beta_second) * gradient * gradient
    first_fix = 1.0 - beta_first**step_count
    second_fix = 1.0 - beta_second**step_count
    update = moment_new / first_fix / (jnp.sqrt(variance_new / second_fix) + epsilon)
    return master - learn_rate * (update + weight_decay * master)


def dot0(left, right):
    return lax.dot_general(left, right, (((0,), (0,)), ((), ())), preferred_element_type=f32)


def spot_of(*axes):
    return tuple(lax.axis_index(a) for a in axes)


def masked_blocks(counts, hid_ref, masked):
    live = lax.broadcasted_iota(jnp.int32, (SLOT, HID), 0) < counts[0, 0]
    masked[...] = jnp.where(live, hid_ref[...], jnp.zeros_like(hid_ref))

    def block(chip, which):
        start = pl.multiple_of((chip * 2 + which) * 128, 128)
        return masked[:, pl.ds(start, 128)]

    return block


def nearest(j):
    return j + 1 - 2 * lax.rem(j, 2), 3 - j, lax.rem(j + 2, 4)


def pack_kernel(counts, hid_ref, cot_ref, to_a, to_b, own_ref, masked, sems):
    j, core = spot_of("zh", "co")
    other = 1 - core
    near_a, near_b, across = nearest(j)
    copies = [
        pltpu.make_async_copy(
            cot_ref.at[:, n * HALF : (n + 1) * HALF], to.at[:, :HALF], sems.at[n]
        )
        for n, to in enumerate((to_a, to_b))
    ]
    for copy in copies:
        copy.start()
    block = masked_blocks(counts, hid_ref, masked)
    for to, near in ((to_a, near_a), (to_b, near_b)):
        for n, (chip, which) in enumerate(
            ((near, core), (across, core), (near, other), (across, other))
        ):
            to[:, HALF + n * 128 : HALF + (n + 1) * 128] = block(chip, which)
    for n, chip in enumerate((j, near_b, j, near_a)):
        own_ref[:, n * 128 : (n + 1) * 128] = block(chip, core)
    for copy in copies:
        copy.wait()


def sibling_kernel(counts, hid_ref, cot_ref, out_ref, masked, sems):
    j, core = spot_of("zh", "co")
    near_a, near_b, _ = nearest(j)
    copy = pltpu.make_async_copy(cot_ref, out_ref.at[:, :DW], sems.at[0])
    copy.start()
    block = masked_blocks(counts, hid_ref, masked)
    for n, chip in enumerate((j, near_b, j, near_a)):
        out_ref[:, DW + n * 128 : DW + (n + 1) * 128] = block(chip, 1 - core)
    copy.wait()


def part_copies(lay_ref, ref, side, sems):
    j = lax.axis_index("zh")
    copies = []
    for n in range(4):
        start = pl.multiple_of((2 * lax.rem(j + n, 4) + side) * PART, 128)
        copies.append(
            pltpu.make_async_copy(
                lay_ref.at[:, pl.ds(start, PART)],
                ref.at[:, n * PART : (n + 1) * PART],
                sems.at[n],
            )
        )
    return copies


def dense_pack_kernel(lay_ref, cot_ref, out_ref, cot, sems):
    last = pltpu.make_async_copy(cot_ref, cot, sems.at[4])
    last.start()
    copies = part_copies(lay_ref, out_ref, 1 - lax.axis_index("co"), sems)
    for copy in copies:
        copy.start()
    last.wait()
    out_ref[:, 4 * PART : 4 * PART + KV] = cot[...].T
    out_ref[:, 4 * PART + KV :] = jnp.zeros((SLOT, 64), bf16)
    for copy in copies:
        copy.wait()


def whole(shape):
    return pl.BlockSpec(shape, lambda *_: (0,) * len(shape))


def in_vmem(kernel, outs, *args, scratch=(), far=(), vmem=VMEM, cost=None):
    specs = [
        pl.BlockSpec(
            memory_space=pltpu.SMEM if a.dtype == jnp.int32 else pltpu.HBM if n in far else pltpu.VMEM
        )
        for n, a in enumerate(args)
    ]
    return pl.pallas_call(
        kernel,
        out_shape=[jax.ShapeDtypeStruct(shape, dtype) for shape, dtype in outs],
        in_specs=specs,
        out_specs=[pl.BlockSpec(memory_space=pltpu.VMEM)] * len(outs),
        scratch_shapes=scratch,
        cost_estimate=cost,
        compiler_params=pltpu.CompilerParams(vmem_limit_bytes=vmem),
    )(*args)


def far_kernel(near_a, near_b, first, rest):
    for n, near in enumerate((near_a, near_b)):
        at = n * (LEAD + 256)
        first[:, at : at + LEAD] = near[:, :LEAD]
        first[:, at + LEAD : at + LEAD + 256] = near[:, HALF + 256 :]
        rest[:, n * REST : n * REST + REST] = near[:, LEAD:HALF]


def products_kernel(first, cot, own, sib, near_a, near_b, far, columns, to_a, to_b, keep):
    width = to_a.shape[1]
    for n, (near, send) in enumerate(((near_a, to_a), (near_b, to_b))):
        at = n * HALF + first
        there = n * (columns.shape[1] // 2)
        factors = n * (LEAD + 256) + LEAD
        h = jnp.concatenate(
            [
                own[:, n * 256 : n * 256 + 256],
                sib[:, DW + n * 256 : DW + n * 256 + 256],
                near[:, HALF : HALF + 256],
                far[:, factors : factors + 256],
            ]
        )
        c = jnp.concatenate(
            [cot[:, at : at + width], sib[:, at : at + width], near[:, first : first + width],
             columns[:, there : there + width]]
        )
        result = dot0(h, c)
        keep[n] = result[:SLOT]
        send[...] = result[SLOT:].astype(bf16)


def expert_products(first, width, *args):
    outs = [((SLOT, width), bf16)] * 2 + [((2, SLOT, width), f32)]
    return in_vmem(functools.partial(products_kernel, first), outs, *args)


def expert_adam_kernel(keep0, keep1, a0, a1, b0, b1, master, moment, variance, out):
    for half, parts in enumerate(((a0, a1), (b0, b1))):

        @pl.when(pl.program_id(0) == half)
        def _(parts=parts):
            for at, keep, got in zip(
                (slice(0, LEAD), slice(LEAD, HALF)), (keep0, keep1), parts
            ):
                gradient = keep[0] + got[...].astype(f32)
                out[:, at] = adam_step(master[:, at], moment[:, at], variance[:, at], gradient)


def expert_adam(keeps, got, master, moment, variance):
    wide = pl.BlockSpec((SLOT, HALF), lambda n: (0, n))
    return pl.pallas_call(
        expert_adam_kernel,
        grid=(2,),
        out_shape=jax.ShapeDtypeStruct((SLOT, DW), f32),
        in_specs=[
            *[pl.BlockSpec((1, SLOT, k.shape[2]), lambda n: (n, 0, 0)) for k in keeps],
            *[pl.BlockSpec(g.shape, lambda n: (0, 0)) for g in got],
            wide, wide, wide,
        ],
        out_specs=wide,
        compiler_params=pltpu.CompilerParams(vmem_limit_bytes=VMEM),
    )(*keeps, *got, master, moment, variance)


def order_kernel(lay_ref, order, own_ref, sems):
    core, low, x, y = spot_of("co", "zl", "x", "y")
    copies = part_copies(lay_ref, own_ref, core, sems)
    for copy in copies:
        copy.start()
    place = lax.broadcasted_iota(jnp.int32, (1, 1024), 1)
    first = (place // 256 + x + core * (y - x)) % 4
    second = (place // 64 % 4 + y + core * (x - y)) % 4
    half = (place // 32 % 2 + low) % 2
    row = place % PAD
    spot = half * 448 + first * (112 - 84 * core) + second * (28 + 84 * core) + row
    spot = jnp.where(row < ROWS, spot, -1)
    rows = lax.broadcasted_iota(jnp.int32, (PART, 1024), 0)
    order[...] = jnp.where(rows == spot, 1.0, 0.0).astype(bf16)
    for copy in copies:
        copy.wait()


def permute_kernel(order, own, to_core, got, *outs):
    for n in range(4):
        part = slice(n * PART, (n + 1) * PART)
        tokens = jnp.concatenate([own[:, part], got[:, part]])
        moved = jnp.dot(tokens, order[...], preferred_element_type=f32).astype(bf16)
        for k, out in enumerate(outs):
            out[:, n * 256 : n * 256 + 256] = moved[:, k * 256 : k * 256 + 256]
    for out in outs:
        out[:SLOT, 1024:] = to_core[:, 4 * PART :]
        out[SLOT:, 1024:] = got[:, 4 * PART :]


def dense_product_kernel(b0, b1, b2, b3, keep, up, across, down):
    blocks = (b0, b1, b2, b3)
    grads = jnp.concatenate([b[:, 1024 : 1024 + KV] for b in blocks])
    for n in range(4):
        tokens = jnp.concatenate([b[:, n * 256 : n * 256 + 256] for b in blocks])
        result = dot0(tokens, grads)
        keep[n] = result[:64]
        for k, out in enumerate((up, across, down)):
            out[n] = result[64 * k + 64 : 64 * k + 128].astype(bf16)


def after_kernel(*refs):
    pass


def after(values, *others):
    return pl.pallas_call(
        after_kernel,
        out_shape=jax.ShapeDtypeStruct(values.shape, values.dtype),
        in_specs=[pl.BlockSpec(memory_space=pltpu.VMEM)] * (1 + len(others)),
        out_specs=pl.BlockSpec(memory_space=pltpu.VMEM),
        input_output_aliases={0: 0},
        cost_estimate=LONG,
        compiler_params=pltpu.CompilerParams(vmem_limit_bytes=VMEM),
    )(values, *others)


def plane_pairs(stage, step):
    pairs = []
    for core in range(2):
        for x in range(4):
            for y in range(4):
                along_x = (core + stage) % 2 == 0
                to = ((x + step) % 4, y) if along_x else (x, (y + step) % 4)
                pairs.append((core * 16 + x * 4 + y, core * 16 + to[0] * 4 + to[1]))
    return pairs


def add(*terms):
    return functools.reduce(lambda a, b: a + b, [t.astype(f32) for t in terms])


def tie(values, *others):
    return lax.optimization_barrier((values, others))[0]


def on_device(
    expert_inputs,
    expert_cotangent,
    row_counts,
    expert_master,
    expert_moment,
    expert_variance,
    layer_inputs,
    layer_cotangent,
    dense_master,
    dense_moment,
    dense_variance,
):
    hid, cot = expert_inputs[0], expert_cotangent[0]
    swap = [(0, 1), (1, 0)]

    (to_core,) = in_vmem(
        dense_pack_kernel,
        [((SLOT, 4224), bf16)],
        layer_inputs,
        layer_cotangent.T,
        scratch=[pltpu.VMEM((KV, SLOT), bf16), pltpu.SemaphoreType.DMA((5,))],
        far=(0, 1),
        vmem=56 * 1024 * 1024,
    )
    dense_got = lax.ppermute(to_core, "co", swap)
    order, own_part = in_vmem(
        order_kernel,
        [((PART, 1024), bf16), ((SLOT, 4 * PART), bf16)],
        layer_inputs,
        scratch=[pltpu.SemaphoreType.DMA((4,))],
        far=(0,),
    )

    to_a, to_b, own = in_vmem(
        pack_kernel,
        [((SLOT, w), bf16) for w in (2304, 2304, 512)],
        row_counts,
        hid,
        cot,
        scratch=[pltpu.VMEM((SLOT, HID), bf16), pltpu.SemaphoreType.DMA((2,))],
        far=(2,),
    )
    near_a = lax.ppermute(to_a, "zh", PAIR_A)
    near_b = lax.ppermute(to_b, "zh", PAIR_B)
    (to_sib,) = in_vmem(
        sibling_kernel,
        [((SLOT, DW + 512), bf16)],
        row_counts,
        hid,
        cot,
        scratch=[pltpu.VMEM((SLOT, HID), bf16), pltpu.SemaphoreType.DMA((1,))],
        far=(2,),
    )
    sib = lax.ppermute(to_sib, "co", swap)

    axes = ("co", "x", "y")
    blocks = list(
        in_vmem(permute_kernel, [((256, 1664), bf16)] * 4, order, own_part, to_core, dense_got)
    )
    blocks = [blocks[0]] + [
        lax.ppermute(blocks[step], axes, plane_pairs(0, step)) for step in (2, 1, 3)
    ]
    keep, up, across, down = in_vmem(
        dense_product_kernel, [((4, 64, KV), f32)] + [((4, 64, KV), bf16)] * 3, *blocks
    )

    to_far, to_far_rest = in_vmem(
        far_kernel,
        [((SLOT, 2 * LEAD + 512), bf16), ((SLOT, 2 * REST), bf16)],
        near_a,
        near_b,
        cost=FAR_COST,
    )
    far = lax.ppermute(tie(to_far, *blocks[1:]), "co", swap)
    mine_too = cot, own, sib, near_a, near_b
    p_a, p_b, keep_p = expert_products(0, LEAD, *mine_too, far, far)
    p_a, p_b = tie((p_a, p_b), keep)
    p_a, p_b = lax.ppermute(p_a, "zh", PAIR_B), lax.ppermute(p_b, "zh", PAIR_A)
    rest = lax.ppermute(to_far_rest, "co", swap)
    q_a, q_b, keep_q = expert_products(LEAD, REST, *mine_too, far, rest)
    keep = tie(keep, q_a)
    q_a, q_b = lax.ppermute(q_a, "zh", PAIR_B), lax.ppermute(q_b, "zh", PAIR_A)

    up, across, down = tie((up, across, down), rest)
    terms = [
        lax.ppermute(block, axes, plane_pairs(1, step))
        for step, block in ((2, across), (1, up), (3, down))
    ]
    line = add(after(keep, p_a, p_b), *terms).reshape(4, 2, PAD, KV)

    mine = line[:, 0] + lax.ppermute(line[:, 1].astype(bf16), "zl", swap).astype(f32)
    dense_grad = mine[0]
    for step in (2, 1, 3):
        term = lax.ppermute(mine[step].astype(bf16), "zh", [(i, (i + step) % 4) for i in range(4)])
        dense_grad = dense_grad + term.astype(f32)
    dense_updated = adam_step(dense_master, dense_moment, dense_variance, dense_grad[:ROWS])

    expert_updated = expert_adam(
        (keep_p, tie(keep_q, dense_updated)), (p_a, q_a, p_b, q_b), expert_master[0], expert_moment[0], expert_variance[0]
    )
    return (expert_updated[None], dense_updated)


def solution(mesh):
    fine = Mesh(mesh.devices.reshape(4, 2, 2, 4, 4), ("zh", "co", "zl", "x", "y"))
    ep, rep = ("zl", "x", "y"), ("zh", "co")
    expert = P(ep, rep, None)
    dense = P(rep + ep, None)
    in_specs = (expert, expert, P(ep, rep)) + (expert,) * 3 + (dense,) * 5
    return jax.shard_map(
        on_device, mesh=fine, in_specs=in_specs, out_specs=(expert, dense), check_vma=False
    )
```

```python
import functools
import jax
import jax.numpy as jnp
from jax import lax
from jax.experimental import pallas as pl
from jax.experimental.pallas import tpu as pltpu
from jax.sharding import Mesh, PartitionSpec as P

beta_first = 0.9
beta_second = 0.999
step_count = 1000.0
learn_rate = 0.05
weight_decay = 0.1
epsilon = 1e-08

SLOT = 128
HID = 1024
DW = 3584
HALF = 1792
LEAD = 1152
REST = HALF - LEAD
D = 7168
KV = 576
PART = 896
ROWS = 28
PAD = 32
bf16, f32 = jnp.bfloat16, jnp.float32

PAIR_A = [(0, 1), (1, 0), (2, 3), (3, 2)]
PAIR_B = [(0, 3), (3, 0), (1, 2), (2, 1)]
VMEM = 24 * 1024 * 1024
LONG = pl.CostEstimate(flops=10_000_000_000, bytes_accessed=4_000_000, transcendentals=0)
FAR_COST = pl.CostEstimate(flops=6_000_000_000, bytes_accessed=4_000_000, transcendentals=0)


def adam_step(master, moment, variance, gradient):
    moment_new = beta_first * moment + (1.0 - beta_first) * gradient
    variance_new = beta_second * variance + (1.0 - beta_second) * gradient * gradient
    first_fix = 1.0 - beta_first**step_count
    second_fix = 1.0 - beta_second**step_count
    update = moment_new / first_fix / (jnp.sqrt(variance_new / second_fix) + epsilon)
    return master - learn_rate * (update + weight_decay * master)


def dot0(left, right):
    return lax.dot_general(left, right, (((0,), (0,)), ((), ())), preferred_element_type=f32)


def spot_of(*axes):
    return tuple(lax.axis_index(a) for a in axes)


def masked_blocks(counts, hid_ref, masked):
    live = lax.broadcasted_iota(jnp.int32, (SLOT, HID), 0) < counts[0, 0]
    masked[...] = jnp.where(live, hid_ref[...], jnp.zeros_like(hid_ref))

    def block(chip, which):
        start = pl.multiple_of((chip * 2 + which) * 128, 128)
        return masked[:, pl.ds(start, 128)]

    return block


def nearest(j):
    return j + 1 - 2 * lax.rem(j, 2), 3 - j, lax.rem(j + 2, 4)


def pack_kernel(counts, hid_ref, cot_ref, to_a, to_b, own_ref, masked, sems):
    j, core = spot_of("zh", "co")
    other = 1 - core
    near_a, near_b, across = nearest(j)
    copies = [
        pltpu.make_async_copy(
            cot_ref.at[:, n * HALF : (n + 1) * HALF], to.at[:, :HALF], sems.at[n]
        )
        for n, to in enumerate((to_a, to_b))
    ]
    for copy in copies:
        copy.start()
    block = masked_blocks(counts, hid_ref, masked)
    for to, near in ((to_a, near_a), (to_b, near_b)):
        for n, (chip, which) in enumerate(
            ((near, core), (across, core), (near, other), (across, other))
        ):
            to[:, HALF + n * 128 : HALF + (n + 1) * 128] = block(chip, which)
    for n, chip in enumerate((j, near_b, j, near_a)):
        own_ref[:, n * 128 : (n + 1) * 128] = block(chip, core)
    for copy in copies:
        copy.wait()


def sibling_kernel(counts, hid_ref, cot_ref, out_ref, masked, sems):
    j, core = spot_of("zh", "co")
    near_a, near_b, _ = nearest(j)
    copy = pltpu.make_async_copy(cot_ref, out_ref.at[:, :DW], sems.at[0])
    copy.start()
    block = masked_blocks(counts, hid_ref, masked)
    for n, chip in enumerate((j, near_b, j, near_a)):
        out_ref[:, DW + n * 128 : DW + (n + 1) * 128] = block(chip, 1 - core)
    copy.wait()


def part_copies(lay_ref, ref, side, sems):
    j = lax.axis_index("zh")
    copies = []
    for n in range(4):
        start = pl.multiple_of((2 * lax.rem(j + n, 4) + side) * PART, 128)
        copies.append(
            pltpu.make_async_copy(
                lay_ref.at[:, pl.ds(start, PART)],
                ref.at[:, n * PART : (n + 1) * PART],
                sems.at[n],
            )
        )
    return copies


def dense_pack_kernel(lay_ref, cot_ref, out_ref, cot, sems):
    last = pltpu.make_async_copy(cot_ref, cot, sems.at[4])
    last.start()
    copies = part_copies(lay_ref, out_ref, 1 - lax.axis_index("co"), sems)
    for copy in copies:
        copy.start()
    last.wait()
    out_ref[:, 4 * PART : 4 * PART + KV] = cot[...].T
    out_ref[:, 4 * PART + KV :] = jnp.zeros((SLOT, 64), bf16)
    for copy in copies:
        copy.wait()


def whole(shape):
    return pl.BlockSpec(shape, lambda *_: (0,) * len(shape))


def in_vmem(kernel, outs, *args, scratch=(), far=(), vmem=VMEM, cost=None):
    specs = [
        pl.BlockSpec(
            memory_space=pltpu.SMEM if a.dtype == jnp.int32 else pltpu.HBM if n in far else pltpu.VMEM
        )
        for n, a in enumerate(args)
    ]
    return pl.pallas_call(
        kernel,
        out_shape=[jax.ShapeDtypeStruct(shape, dtype) for shape, dtype in outs],
        in_specs=specs,
        out_specs=[pl.BlockSpec(memory_space=pltpu.VMEM)] * len(outs),
        scratch_shapes=scratch,
        cost_estimate=cost,
        compiler_params=pltpu.CompilerParams(vmem_limit_bytes=vmem),
    )(*args)


def far_kernel(near_a, near_b, first, rest):
    for n, near in enumerate((near_a, near_b)):
        at = n * (LEAD + 256)
        first[:, at : at + LEAD] = near[:, :LEAD]
        first[:, at + LEAD : at + LEAD + 256] = near[:, HALF + 256 :]
        rest[:, n * REST : n * REST + REST] = near[:, LEAD:HALF]


def products_kernel(first, cot, own, sib, near_a, near_b, far, columns, to_a, to_b, keep):
    width = to_a.shape[1]
    for n, (near, send) in enumerate(((near_a, to_a), (near_b, to_b))):
        at = n * HALF + first
        there = n * (columns.shape[1] // 2)
        factors = n * (LEAD + 256) + LEAD
        h = jnp.concatenate(
            [
                own[:, n * 256 : n * 256 + 256],
                sib[:, DW + n * 256 : DW + n * 256 + 256],
                near[:, HALF : HALF + 256],
                far[:, factors : factors + 256],
            ]
        )
        c = jnp.concatenate(
            [cot[:, at : at + width], sib[:, at : at + width], near[:, first : first + width],
             columns[:, there : there + width]]
        )
        result = dot0(h, c)
        keep[n] = result[:SLOT]
        send[...] = result[SLOT:].astype(bf16)


def expert_products(first, width, *args):
    outs = [((SLOT, width), bf16)] * 2 + [((2, SLOT, width), f32)]
    return in_vmem(functools.partial(products_kernel, first), outs, *args)


def expert_adam_kernel(keep0, keep1, a0, a1, b0, b1, master, moment, variance, _, out):
    for half, parts in enumerate(((a0, a1), (b0, b1))):

        @pl.when(pl.program_id(0) == half)
        def _(parts=parts):
            for at, keep, got in zip(
                (slice(0, LEAD), slice(LEAD, HALF)), (keep0, keep1), parts
            ):
                gradient = keep[0] + got[...].astype(f32)
                out[:, at] = adam_step(master[:, at], moment[:, at], variance[:, at], gradient)


def expert_adam(keeps, got, master, moment, variance, last):
    wide = pl.BlockSpec((SLOT, HALF), lambda n: (0, n))
    return pl.pallas_call(
        expert_adam_kernel,
        grid=(2,),
        out_shape=jax.ShapeDtypeStruct((SLOT, DW), f32),
        in_specs=[
            *[pl.BlockSpec((1, SLOT, k.shape[2]), lambda n: (n, 0, 0)) for k in keeps],
            *[pl.BlockSpec(g.shape, lambda n: (0, 0)) for g in got],
            wide, wide, wide, pl.BlockSpec(last.shape, lambda n: (0, 0)),
        ],
        out_specs=wide,
        cost_estimate=LONG,
        compiler_params=pltpu.CompilerParams(vmem_limit_bytes=VMEM),
    )(*keeps, *got, master, moment, variance, last)


def order_kernel(lay_ref, order, own_ref, sems):
    core, low, x, y = spot_of("co", "zl", "x", "y")
    copies = part_copies(lay_ref, own_ref, core, sems)
    for copy in copies:
        copy.start()
    place = lax.broadcasted_iota(jnp.int32, (1, 1024), 1)
    first = (place // 256 + x + core * (y - x)) % 4
    second = (place // 64 % 4 + y + core * (x - y)) % 4
    half = (place // 32 % 2 + low) % 2
    row = place % PAD
    spot = half * 448 + first * (112 - 84 * core) + second * (28 + 84 * core) + row
    spot = jnp.where(row < ROWS, spot, -1)
    rows = lax.broadcasted_iota(jnp.int32, (PART, 1024), 0)
    order[...] = jnp.where(rows == spot, 1.0, 0.0).astype(bf16)
    for copy in copies:
        copy.wait()


def permute_kernel(order, own, to_core, got, *outs):
    for n in range(4):
        part = slice(n * PART, (n + 1) * PART)
        tokens = jnp.concatenate([own[:, part], got[:, part]])
        moved = jnp.dot(tokens, order[...], preferred_element_type=f32).astype(bf16)
        for k, out in enumerate(outs):
            out[:, n * 256 : n * 256 + 256] = moved[:, k * 256 : k * 256 + 256]
    for out in outs:
        out[:SLOT, 1024:] = to_core[:, 4 * PART :]
        out[SLOT:, 1024:] = got[:, 4 * PART :]


def dense_product_kernel(b0, b1, b2, b3, keep, up, across, down):
    blocks = (b0, b1, b2, b3)
    grads = jnp.concatenate([b[:, 1024 : 1024 + KV] for b in blocks])
    for n in range(4):
        tokens = jnp.concatenate([b[:, n * 256 : n * 256 + 256] for b in blocks])
        result = dot0(tokens, grads)
        keep[n] = result[:64]
        for k, out in enumerate((up, across, down)):
            out[n] = result[64 * k + 64 : 64 * k + 128].astype(bf16)


def after_kernel(*refs):
    pass


def after(values, *others):
    return pl.pallas_call(
        after_kernel,
        out_shape=jax.ShapeDtypeStruct(values.shape, values.dtype),
        in_specs=[pl.BlockSpec(memory_space=pltpu.VMEM)] * (1 + len(others)),
        out_specs=pl.BlockSpec(memory_space=pltpu.VMEM),
        input_output_aliases={0: 0},
        cost_estimate=LONG,
        compiler_params=pltpu.CompilerParams(vmem_limit_bytes=VMEM),
    )(values, *others)


def plane_pairs(stage, step):
    pairs = []
    for core in range(2):
        for x in range(4):
            for y in range(4):
                along_x = (core + stage) % 2 == 0
                to = ((x + step) % 4, y) if along_x else (x, (y + step) % 4)
                pairs.append((core * 16 + x * 4 + y, core * 16 + to[0] * 4 + to[1]))
    return pairs


def add(*terms):
    return functools.reduce(lambda a, b: a + b, [t.astype(f32) for t in terms])


def tie(values, *others):
    return lax.optimization_barrier((values, others))[0]


def on_device(
    expert_inputs,
    expert_cotangent,
    row_counts,
    expert_master,
    expert_moment,
    expert_variance,
    layer_inputs,
    layer_cotangent,
    dense_master,
    dense_moment,
    dense_variance,
):
    hid, cot = expert_inputs[0], expert_cotangent[0]
    swap = [(0, 1), (1, 0)]

    (to_core,) = in_vmem(
        dense_pack_kernel,
        [((SLOT, 4224), bf16)],
        layer_inputs,
        layer_cotangent.T,
        scratch=[pltpu.VMEM((KV, SLOT), bf16), pltpu.SemaphoreType.DMA((5,))],
        far=(0, 1),
        vmem=56 * 1024 * 1024,
    )
    dense_got = lax.ppermute(to_core, "co", swap)
    order, own_part = in_vmem(
        order_kernel,
        [((PART, 1024), bf16), ((SLOT, 4 * PART), bf16)],
        layer_inputs,
        scratch=[pltpu.SemaphoreType.DMA((4,))],
        far=(0,),
    )

    to_a, to_b, own = in_vmem(
        pack_kernel,
        [((SLOT, w), bf16) for w in (2304, 2304, 512)],
        row_counts,
        hid,
        cot,
        scratch=[pltpu.VMEM((SLOT, HID), bf16), pltpu.SemaphoreType.DMA((2,))],
        far=(2,),
    )
    near_a = lax.ppermute(to_a, "zh", PAIR_A)
    near_b = lax.ppermute(to_b, "zh", PAIR_B)
    (to_sib,) = in_vmem(
        sibling_kernel,
        [((SLOT, DW + 512), bf16)],
        row_counts,
        hid,
        cot,
        scratch=[pltpu.VMEM((SLOT, HID), bf16), pltpu.SemaphoreType.DMA((1,))],
        far=(2,),
    )
    sib = lax.ppermute(to_sib, "co", swap)

    axes = ("co", "x", "y")
    blocks = list(
        in_vmem(permute_kernel, [((256, 1664), bf16)] * 4, order, own_part, to_core, dense_got)
    )
    blocks = [blocks[0]] + [
        lax.ppermute(blocks[step], axes, plane_pairs(0, step)) for step in (2, 1, 3)
    ]
    keep, up, across, down = in_vmem(
        dense_product_kernel, [((4, 64, KV), f32)] + [((4, 64, KV), bf16)] * 3, *blocks
    )

    to_far, to_far_rest = in_vmem(
        far_kernel,
        [((SLOT, 2 * LEAD + 512), bf16), ((SLOT, 2 * REST), bf16)],
        near_a,
        near_b,
        cost=FAR_COST,
    )
    far = lax.ppermute(tie(to_far, *blocks[1:]), "co", swap)
    mine_too = cot, own, sib, near_a, near_b
    p_a, p_b, keep_p = expert_products(0, LEAD, *mine_too, far, far)
    p_a, p_b = tie((p_a, p_b), keep)
    p_a, p_b = lax.ppermute(p_a, "zh", PAIR_B), lax.ppermute(p_b, "zh", PAIR_A)
    rest = lax.ppermute(to_far_rest, "co", swap)
    q_a, q_b, keep_q = expert_products(LEAD, REST, *mine_too, far, rest)
    keep = tie(keep, q_a)
    q_a, q_b = lax.ppermute(q_a, "zh", PAIR_B), lax.ppermute(q_b, "zh", PAIR_A)

    up, across, down = tie((up, across, down), rest)
    terms = [
        lax.ppermute(block, axes, plane_pairs(1, step))
        for step, block in ((2, across), (1, up), (3, down))
    ]
    line = add(after(keep, p_a, p_b), *terms).reshape(4, 2, PAD, KV)

    mine = line[0]
    for step in (2, 1, 3):
        term = lax.ppermute(line[step].astype(bf16), "zh", [(i, (i + step) % 4) for i in range(4)])
        mine = mine + term.astype(f32)
    theirs = mine[1].astype(bf16)
    dense_grad = mine[0] + lax.ppermute(theirs, "zl", swap).astype(f32)
    dense_updated = adam_step(dense_master, dense_moment, dense_variance, dense_grad[:ROWS])

    last = lax.ppermute(q_a[:16, :128] + q_b[:16, :128], "co", swap)
    state = expert_master[0], expert_moment[0], expert_variance[0]
    keeps = keep_p, tie(keep_q, theirs)
    expert_updated = expert_adam(keeps, (p_a, q_a, p_b, q_b), *state, last)
    return (expert_updated[None], dense_updated)


def solution(mesh):
    fine = Mesh(mesh.devices.reshape(4, 2, 2, 4, 4), ("zh", "co", "zl", "x", "y"))
    ep, rep = ("zl", "x", "y"), ("zh", "co")
    expert = P(ep, rep, None)
    dense = P(rep + ep, None)
    in_specs = (expert, expert, P(ep, rep)) + (expert,) * 3 + (dense,) * 5
    return jax.shard_map(
        on_device, mesh=fine, in_specs=in_specs, out_specs=(expert, dense), check_vma=False
    )
```

```python
import functools
import jax
import jax.numpy as jnp
from jax import lax
from jax.experimental import pallas as pl
from jax.experimental.pallas import tpu as pltpu
from jax.sharding import Mesh, PartitionSpec as P

beta_first = 0.9
beta_second = 0.999
step_count = 1000.0
learn_rate = 0.05
weight_decay = 0.1
epsilon = 1e-08

SLOT = 128
HID = 1024
DW = 3584
HALF = 1792
LEAD = 1152
REST = HALF - LEAD
D = 7168
KV = 576
PART = 896
ROWS = 28
PAD = 32
bf16, f32 = jnp.bfloat16, jnp.float32

PAIR_A = [(0, 1), (1, 0), (2, 3), (3, 2)]
PAIR_B = [(0, 3), (3, 0), (1, 2), (2, 1)]
VMEM = 24 * 1024 * 1024
LONG = pl.CostEstimate(flops=10_000_000_000, bytes_accessed=4_000_000, transcendentals=0)
FAR_COST = pl.CostEstimate(flops=6_000_000_000, bytes_accessed=4_000_000, transcendentals=0)


def adam_step(master, moment, variance, gradient):
    moment_new = beta_first * moment + (1.0 - beta_first) * gradient
    variance_new = beta_second * variance + (1.0 - beta_second) * gradient * gradient
    first_fix = 1.0 - beta_first**step_count
    second_fix = 1.0 - beta_second**step_count
    update = moment_new / first_fix / (jnp.sqrt(variance_new / second_fix) + epsilon)
    return master - learn_rate * (update + weight_decay * master)


def dot0(left, right):
    return lax.dot_general(left, right, (((0,), (0,)), ((), ())), preferred_element_type=f32)


def spot_of(*axes):
    return tuple(lax.axis_index(a) for a in axes)


def masked_blocks(counts, hid_ref, masked):
    live = lax.broadcasted_iota(jnp.int32, (SLOT, HID), 0) < counts[0, 0]
    masked[...] = jnp.where(live, hid_ref[...], jnp.zeros_like(hid_ref))

    def block(chip, which):
        start = pl.multiple_of((chip * 2 + which) * 128, 128)
        return masked[:, pl.ds(start, 128)]

    return block


def nearest(j):
    return j + 1 - 2 * lax.rem(j, 2), 3 - j, lax.rem(j + 2, 4)


def pack_kernel(counts, hid_ref, cot_ref, to_a, to_b, own_ref, masked, sems):
    j, core = spot_of("zh", "co")
    other = 1 - core
    near_a, near_b, across = nearest(j)
    copies = [
        pltpu.make_async_copy(
            cot_ref.at[:, n * HALF : (n + 1) * HALF], to.at[:, :HALF], sems.at[n]
        )
        for n, to in enumerate((to_a, to_b))
    ]
    for copy in copies:
        copy.start()
    block = masked_blocks(counts, hid_ref, masked)
    for to, near in ((to_a, near_a), (to_b, near_b)):
        for n, (chip, which) in enumerate(
            ((near, core), (across, core), (near, other), (across, other))
        ):
            to[:, HALF + n * 128 : HALF + (n + 1) * 128] = block(chip, which)
    for n, chip in enumerate((j, near_b, j, near_a)):
        own_ref[:, n * 128 : (n + 1) * 128] = block(chip, core)
    for copy in copies:
        copy.wait()


def sibling_kernel(counts, hid_ref, cot_ref, out_ref, masked, sems):
    j, core = spot_of("zh", "co")
    near_a, near_b, _ = nearest(j)
    copy = pltpu.make_async_copy(cot_ref, out_ref.at[:, :DW], sems.at[0])
    copy.start()
    block = masked_blocks(counts, hid_ref, masked)
    for n, chip in enumerate((j, near_b, j, near_a)):
        out_ref[:, DW + n * 128 : DW + (n + 1) * 128] = block(chip, 1 - core)
    copy.wait()


def ring_place(me, step):
    return (me + step * (1 + 2 * (me % 2))) % 4


def part_copies(lay_ref, ref, side, sems):
    j = lax.axis_index("zh")
    copies = []
    for n in range(4):
        start = pl.multiple_of((2 * ring_place(j, n) + side) * PART, 128)
        copies.append(
            pltpu.make_async_copy(
                lay_ref.at[:, pl.ds(start, PART)],
                ref.at[:, n * PART : (n + 1) * PART],
                sems.at[n],
            )
        )
    return copies


def dense_pack_kernel(lay_ref, cot_ref, out_ref, cot, sems):
    last = pltpu.make_async_copy(cot_ref, cot, sems.at[4])
    last.start()
    copies = part_copies(lay_ref, out_ref, 1 - lax.axis_index("co"), sems)
    for copy in copies:
        copy.start()
    last.wait()
    out_ref[:, 4 * PART : 4 * PART + KV] = cot[...].T
    out_ref[:, 4 * PART + KV :] = jnp.zeros((SLOT, 64), bf16)
    for copy in copies:
        copy.wait()


def whole(shape):
    return pl.BlockSpec(shape, lambda *_: (0,) * len(shape))


def in_vmem(kernel, outs, *args, scratch=(), far=(), vmem=VMEM, cost=None):
    specs = [
        pl.BlockSpec(
            memory_space=pltpu.SMEM if a.dtype == jnp.int32 else pltpu.HBM if n in far else pltpu.VMEM
        )
        for n, a in enumerate(args)
    ]
    return pl.pallas_call(
        kernel,
        out_shape=[jax.ShapeDtypeStruct(shape, dtype) for shape, dtype in outs],
        in_specs=specs,
        out_specs=[pl.BlockSpec(memory_space=pltpu.VMEM)] * len(outs),
        scratch_shapes=scratch,
        cost_estimate=cost,
        compiler_params=pltpu.CompilerParams(vmem_limit_bytes=vmem),
    )(*args)


def far_kernel(near_a, near_b, first, rest):
    for n, near in enumerate((near_a, near_b)):
        at = n * (LEAD + 256)
        first[:, at : at + LEAD] = near[:, :LEAD]
        first[:, at + LEAD : at + LEAD + 256] = near[:, HALF + 256 :]
        rest[:, n * REST : n * REST + REST] = near[:, LEAD:HALF]


def products_kernel(first, cot, own, sib, near_a, near_b, far, columns, to_a, to_b, keep):
    width = to_a.shape[1]
    for n, (near, send) in enumerate(((near_a, to_a), (near_b, to_b))):
        at = n * HALF + first
        there = n * (columns.shape[1] // 2)
        factors = n * (LEAD + 256) + LEAD
        h = jnp.concatenate(
            [
                own[:, n * 256 : n * 256 + 256],
                sib[:, DW + n * 256 : DW + n * 256 + 256],
                near[:, HALF : HALF + 256],
                far[:, factors : factors + 256],
            ]
        )
        c = jnp.concatenate(
            [cot[:, at : at + width], sib[:, at : at + width], near[:, first : first + width],
             columns[:, there : there + width]]
        )
        result = dot0(h, c)
        keep[n] = result[:SLOT]
        send[...] = result[SLOT:].astype(bf16)


def expert_products(first, width, *args):
    outs = [((SLOT, width), bf16)] * 2 + [((2, SLOT, width), f32)]
    return in_vmem(functools.partial(products_kernel, first), outs, *args)


def expert_adam_kernel(keep0, keep1, a0, a1, b0, b1, master, moment, variance, _, out):
    for half, parts in enumerate(((a0, a1), (b0, b1))):

        @pl.when(pl.program_id(0) == half)
        def _(parts=parts):
            for at, keep, got in zip(
                (slice(0, LEAD), slice(LEAD, HALF)), (keep0, keep1), parts
            ):
                gradient = keep[0] + got[...].astype(f32)
                out[:, at] = adam_step(master[:, at], moment[:, at], variance[:, at], gradient)


def expert_adam(keeps, got, master, moment, variance, last):
    wide = pl.BlockSpec((SLOT, HALF), lambda n: (0, n))
    return pl.pallas_call(
        expert_adam_kernel,
        grid=(2,),
        out_shape=jax.ShapeDtypeStruct((SLOT, DW), f32),
        in_specs=[
            *[pl.BlockSpec((1, SLOT, k.shape[2]), lambda n: (n, 0, 0)) for k in keeps],
            *[pl.BlockSpec(g.shape, lambda n: (0, 0)) for g in got],
            wide, wide, wide, pl.BlockSpec(last.shape, lambda n: (0, 0)),
        ],
        out_specs=wide,
        cost_estimate=LONG,
        compiler_params=pltpu.CompilerParams(vmem_limit_bytes=VMEM),
    )(*keeps, *got, master, moment, variance, last)


def order_kernel(lay_ref, order, own_ref, sems):
    core, low, x, y = spot_of("co", "zl", "x", "y")
    copies = part_copies(lay_ref, own_ref, core, sems)
    for copy in copies:
        copy.start()
    place = lax.broadcasted_iota(jnp.int32, (1, 1024), 1)
    first = ring_place(x + core * (y - x), place // 256)
    second = ring_place(y + core * (x - y), place // 64 % 4)
    half = (place // 32 % 2 + low) % 2
    row = place % PAD
    spot = half * 448 + first * (112 - 84 * core) + second * (28 + 84 * core) + row
    spot = jnp.where(row < ROWS, spot, -1)
    rows = lax.broadcasted_iota(jnp.int32, (PART, 1024), 0)
    order[...] = jnp.where(rows == spot, 1.0, 0.0).astype(bf16)
    for copy in copies:
        copy.wait()


def permute_kernel(order, own, to_core, got, *outs):
    for n in range(4):
        part = slice(n * PART, (n + 1) * PART)
        tokens = jnp.concatenate([own[:, part], got[:, part]])
        moved = jnp.dot(tokens, order[...], preferred_element_type=f32).astype(bf16)
        for k, out in enumerate(outs):
            out[:, n * 256 : n * 256 + 256] = moved[:, k * 256 : k * 256 + 256]
    for out in outs:
        out[:SLOT, 1024:] = to_core[:, 4 * PART :]
        out[SLOT:, 1024:] = got[:, 4 * PART :]


def dense_product_kernel(b0, b1, b2, b3, keep, up, across, down):
    blocks = (b0, b1, b2, b3)
    grads = jnp.concatenate([b[:, 1024 : 1024 + KV] for b in blocks])
    for n in range(4):
        tokens = jnp.concatenate([b[:, n * 256 : n * 256 + 256] for b in blocks])
        result = dot0(tokens, grads)
        keep[n] = result[:64]
        for k, out in enumerate((up, across, down)):
            out[n] = result[64 * k + 64 : 64 * k + 128].astype(bf16)


def after_kernel(*refs):
    pass


def after(values, *others):
    return pl.pallas_call(
        after_kernel,
        out_shape=jax.ShapeDtypeStruct(values.shape, values.dtype),
        in_specs=[pl.BlockSpec(memory_space=pltpu.VMEM)] * (1 + len(others)),
        out_specs=pl.BlockSpec(memory_space=pltpu.VMEM),
        input_output_aliases={0: 0},
        cost_estimate=LONG,
        compiler_params=pltpu.CompilerParams(vmem_limit_bytes=VMEM),
    )(values, *others)


def plane_pairs(stage, step):
    pairs = []
    for core in range(2):
        for x in range(4):
            for y in range(4):
                along_x = (core + stage) % 2 == 0
                to = (ring_place(x, step), y) if along_x else (x, ring_place(y, step))
                pairs.append((core * 16 + x * 4 + y, core * 16 + to[0] * 4 + to[1]))
    return pairs


def add(*terms):
    return functools.reduce(lambda a, b: a + b, [t.astype(f32) for t in terms])


def tie(values, *others):
    return lax.optimization_barrier((values, others))[0]


def on_device(
    expert_inputs,
    expert_cotangent,
    row_counts,
    expert_master,
    expert_moment,
    expert_variance,
    layer_inputs,
    layer_cotangent,
    dense_master,
    dense_moment,
    dense_variance,
):
    hid, cot = expert_inputs[0], expert_cotangent[0]
    swap = [(0, 1), (1, 0)]

    (to_core,) = in_vmem(
        dense_pack_kernel,
        [((SLOT, 4224), bf16)],
        layer_inputs,
        layer_cotangent.T,
        scratch=[pltpu.VMEM((KV, SLOT), bf16), pltpu.SemaphoreType.DMA((5,))],
        far=(0, 1),
        vmem=56 * 1024 * 1024,
    )
    dense_got = lax.ppermute(to_core, "co", swap)
    order, own_part = in_vmem(
        order_kernel,
        [((PART, 1024), bf16), ((SLOT, 4 * PART), bf16)],
        layer_inputs,
        scratch=[pltpu.SemaphoreType.DMA((4,))],
        far=(0,),
    )

    to_a, to_b, own = in_vmem(
        pack_kernel,
        [((SLOT, w), bf16) for w in (2304, 2304, 512)],
        row_counts,
        hid,
        cot,
        scratch=[pltpu.VMEM((SLOT, HID), bf16), pltpu.SemaphoreType.DMA((2,))],
        far=(2,),
    )
    near_a = lax.ppermute(to_a, "zh", PAIR_A)
    near_b = lax.ppermute(to_b, "zh", PAIR_B)
    (to_sib,) = in_vmem(
        sibling_kernel,
        [((SLOT, DW + 512), bf16)],
        row_counts,
        hid,
        cot,
        scratch=[pltpu.VMEM((SLOT, HID), bf16), pltpu.SemaphoreType.DMA((1,))],
        far=(2,),
    )
    sib = lax.ppermute(to_sib, "co", swap)

    axes = ("co", "x", "y")
    blocks = list(
        in_vmem(permute_kernel, [((256, 1664), bf16)] * 4, order, own_part, to_core, dense_got)
    )
    blocks = [blocks[0]] + [
        lax.ppermute(blocks[step], axes, plane_pairs(0, step)) for step in (2, 1, 3)
    ]
    keep, up, across, down = in_vmem(
        dense_product_kernel, [((4, 64, KV), f32)] + [((4, 64, KV), bf16)] * 3, *blocks
    )

    to_far, to_far_rest = in_vmem(
        far_kernel,
        [((SLOT, 2 * LEAD + 512), bf16), ((SLOT, 2 * REST), bf16)],
        near_a,
        near_b,
        cost=FAR_COST,
    )
    far = lax.ppermute(tie(to_far, *blocks[1:]), "co", swap)
    mine_too = cot, own, sib, near_a, near_b
    p_a, p_b, keep_p = expert_products(0, LEAD, *mine_too, far, far)
    p_a, p_b = tie((p_a, p_b), keep)
    p_a, p_b = lax.ppermute(p_a, "zh", PAIR_B), lax.ppermute(p_b, "zh", PAIR_A)
    rest = lax.ppermute(to_far_rest, "co", swap)
    q_a, q_b, keep_q = expert_products(LEAD, REST, *mine_too, far, rest)
    keep = tie(keep, q_a)
    q_a, q_b = lax.ppermute(q_a, "zh", PAIR_B), lax.ppermute(q_b, "zh", PAIR_A)

    up, across, down = tie((up, across, down), rest)
    terms = [
        lax.ppermute(block, axes, plane_pairs(1, step))
        for step, block in ((2, across), (1, up), (3, down))
    ]
    line = add(after(keep, p_a, p_b), *terms).reshape(4, 2, PAD, KV)

    mine = line[0]
    for step in (1, 3, 2):
        term = lax.ppermute(line[step].astype(bf16), "zh", [(i, ring_place(i, step)) for i in range(4)])
        mine = mine + term.astype(f32)
    theirs = mine[1].astype(bf16)
    dense_grad = mine[0] + lax.ppermute(theirs, "zl", swap).astype(f32)
    dense_updated = adam_step(dense_master, dense_moment, dense_variance, dense_grad[:ROWS])

    last = lax.ppermute(q_a[:16, :128] + q_b[:16, :128], "co", swap)
    state = expert_master[0], expert_moment[0], expert_variance[0]
    keeps = keep_p, tie(keep_q, theirs)
    expert_updated = expert_adam(keeps, (p_a, q_a, p_b, q_b), *state, last)
    return (expert_updated[None], dense_updated)


def solution(mesh):
    fine = Mesh(mesh.devices.reshape(4, 2, 2, 4, 4), ("zh", "co", "zl", "x", "y"))
    ep, rep = ("zl", "x", "y"), ("zh", "co")
    expert = P(ep, rep, None)
    dense = P(rep + ep, None)
    in_specs = (expert, expert, P(ep, rep)) + (expert,) * 3 + (dense,) * 5
    return jax.shard_map(
        on_device, mesh=fine, in_specs=in_specs, out_specs=(expert, dense), check_vma=False
    )
```
